512 devices in a mesh: expert: 64 (over z_lo, y, core), mp: 8 (over x, z_hi).
Axes of the slice: x: 4, y: 8, z: 8 (z_hi: 2, z_lo: 4; z = z_hi * 4 + z_lo), core: 2. Of those that a mesh axis runs over, the one named last changes fastest.
Arguments:
- queries: bfloat16 [16384, 2048], P('expert', 'mp'), may hold values from -8 to 8
- src_keys: bfloat16 [16384, 2048], P(('expert', 'mp')), may hold values from -8 to 8
- src_values: bfloat16 [16384, 2048], P(('expert', 'mp')), may hold values from -9 to 9
- tgt_doc: int32 [64, 256], P('expert'), may hold values from 0 to 3, never falling along the last dimension, each value on 1 to 128 neighbouring positions
- src_doc: int32 [64, 256], P('expert'), may hold values from 0 to 3, never falling along the last dimension, each value on 1 to 128 neighbouring positions
- hidden_in: bfloat16 [16384, 4096], P('expert', 'mp'), may hold values from -6 to 6
- out_proj: bfloat16 [2048, 4096], P('expert', 'mp'), may hold values from -0.375 to 0.375
- norm_gain: float32 [4096], P('mp'), may hold values from 0.1 to 1.9
- router: bfloat16 [4096, 64], P('mp'), may hold values from -0.09375 to 0.09375
- expert_ids: int32 [64, 256], P('expert'), may hold values from 0 to 63, as said below
- expert_slots: int32 [64, 256], P('expert'), may hold values from 0 to 7, as said below
- w_in: bfloat16 [64, 4096, 2048], P('expert', None, 'mp'), may hold values from -0.09375 to 0.09375
- w_out: bfloat16 [64, 2048, 4096], P('expert', 'mp'), may hold values from -0.125 to 0.125
Outputs:
- layer_out: bfloat16 [16384, 4096], P('expert', 'mp')
The draws below stay inside these ranges and needn't reach their ends.
Inputs may be any that keep to these rules, and one draw needn't show every extreme that they name: `expert_ids`: within a group no two rows share an expert and a slot; an expert has at most 8 rows of one group, and one expert has exactly 8 rows of every group. `expert_slots`: slots are numbered within the expert's slots for the group. `tgt_doc`: each group's target rows name every document id from 0 to 3. `src_doc`: each group's source rows name every document id from 0 to 3.
All inputs are finite; a program needn't handle non-finite values.
Results may differ from the reference program's by a relative error of at most 0.011.
Values may be sent and summed in bfloat16 or wider, within the bound.
No kernel may reach another device: no remote copies, remote signals or barrier semaphores. Data moves between devices by JAX's collectives and lax.ppermute only.
A program may use at most 64 MiB of HBM per device.

```python
import math
from functools import reduce
import jax
import jax.numpy as jnp
import numpy as np
from jax import lax

D = 4096
HEADS = 32
HEAD_DIM = 64
FF = 2048
TARGET_GROUP = 256
DOCS = 4
HD = 2048
EXPERTS = 64
GROUPS = 64
SPECIALIST_ROOM = 8
SRC_GRP = 256
TOKENS = 16384
SOURCES = 16384
N_MP = 8


def routing_table(key):
    base = jax.random.fold_in(key, 4242)
    overall_places = EXPERTS * SPECIALIST_ROOM
    preferred_specialist = jax.random.randint(jax.random.fold_in(base, 1), (), 0, EXPERTS)

    def one_group(group_key):
        first_key, second_key = jax.random.split(group_key)
        specialist_rating = jax.random.randint(first_key, (overall_places,), 0, 1 << 18)
        ordinal_location = jnp.arange(overall_places, dtype=jnp.int32)
        rating_increment = jnp.where(ordinal_location // SPECIALIST_ROOM == preferred_specialist, 1 << 19, 0)
        specialist_rating = (specialist_rating + rating_increment) * overall_places + ordinal_location
        unused, chosen = lax.top_k(specialist_rating, TARGET_GROUP)
        order = jax.random.permutation(second_key, TARGET_GROUP)
        return chosen[order]
    group_keys = jax.random.split(jax.random.fold_in(base, 2), GROUPS)
    return jax.vmap(one_group)(group_keys)


def draw_expert_ids(key, part):
    return (routing_table(key) // SPECIALIST_ROOM).astype(jnp.int32)


def draw_expert_slots(key, part):
    return (routing_table(key) % SPECIALIST_ROOM).astype(jnp.int32)


def draw_queries(key, part):
    base = jax.random.normal(jax.random.fold_in(key, 11), (TOKENS, HD), jnp.float32)
    return jnp.clip(base, -8.0, 8.0).astype(jnp.bfloat16)


def draw_src_keys(key, part):
    base = jax.random.normal(jax.random.fold_in(key, 21), (SOURCES, HD), jnp.float32)
    return jnp.clip(base, -8.0, 8.0).astype(jnp.bfloat16)


def spiked(entries, key, source, target, parts, factor):
    def block_of(axis_at):
        return (jnp.arange(entries.shape[axis_at]) // (entries.shape[axis_at] // parts)).reshape((-1,) + (1,) * (entries.ndim - 1 - axis_at))

    one_side = jax.random.permutation(key, parts)[block_of(target)]
    other_side = (block_of(target) + parts // 2) % parts
    return jnp.where((block_of(source) == one_side) | (block_of(source) == other_side), factor * entries, entries)


def steps_of(rng, shape, cuts, least, high):
    factor_of, own = 1.0, jax.random.fold_in(rng, 6)
    for axis_at, shards_of in cuts:
        heights = jnp.exp(jax.random.uniform(jax.random.fold_in(own, axis_at), (shards_of,), jnp.float32, least / len(cuts), high / len(cuts)))
        factor_of = factor_of * jnp.repeat(heights, shape[axis_at] // shards_of).reshape([-1 if axis == axis_at else 1 for axis in range(len(shape))])
    return factor_of


def split_up(count, total, limit, skew):
    weights = [(1 << 20) // math.isqrt(standing ** skew) + 1 for standing in range(2, count + 1)]
    spare, holding = total - limit - (count - 1), [1] * (count - 1)
    while spare > 0:
        free = [i for i in range(count - 1) if holding[i] < limit]
        mass, remaining = sum([weights[i] for i in free]), spare
        for i in free:
            more = min(limit - holding[i], max(1, remaining * weights[i] // mass), spare)
            holding[i] = holding[i] + more
            spare = spare - more
    return np.array([limit] + holding)


def uneven_parts(key, number_of, total, limit, skew):
    if number_of == 2:
        one = jax.random.randint(key, (), max(1, total - limit), min(limit, total - 1) + 1)
        return jnp.stack([one, total - one])
    tallies = jnp.asarray(split_up(number_of, total, limit, skew), jnp.int32)
    pairs = (number_of - 1) // 2
    source_of, receiver = tallies[1:1 + 2 * pairs:2], tallies[2:2 + 2 * pairs:2]
    slack = jnp.minimum(source_of - 1, limit - receiver)
    passed = jax.random.randint(jax.random.fold_in(key, 1), (pairs,), 0, 1 << 20) % (slack + 1)
    tallies = tallies.at[1:1 + 2 * pairs:2].set(source_of - passed).at[2:2 + 2 * pairs:2].set(receiver + passed)
    return tallies[jax.random.permutation(jax.random.fold_in(key, 2), number_of)]


def scatter_about(own_key, dims, deviation, most, cuts=(), held_as=jnp.bfloat16):
    array = deviation * jax.random.normal(own_key, dims, jnp.float32)
    if cuts:
        array = array * steps_of(own_key, dims, cuts, -0.22, 0.18)
    return jnp.clip(array, -most, most).astype(held_as)


def gaussian_with(rng, dims, deviation, reach, cuts, heavy, kind=jnp.bfloat16):
    values = deviation * jax.random.normal(rng, dims, jnp.float32)
    if cuts:
        values = values * steps_of(rng, dims, cuts, -0.22, 0.18)
    return jnp.clip(spiked(values, jax.random.fold_in(rng, 3), *heavy), -reach, reach).astype(kind)


def setup_inputs(seed: int = 0) -> dict:
    keys = jax.random.split(jax.random.key(seed), 14)
    queries = draw_queries(jax.random.fold_in(keys[13], 71), 0)
    src_keys = draw_src_keys(jax.random.fold_in(keys[13], 71), 0)
    src_values = scatter_about(keys[2], (SOURCES, HD), 1.5, 9.0, ((0, 512),))
    tgt_doc = jax.vmap(lambda own: jnp.searchsorted(jnp.cumsum(uneven_parts(own, DOCS, TARGET_GROUP, TARGET_GROUP // 2, 1)), jnp.arange(TARGET_GROUP), side="right"))(jax.random.split(keys[3], GROUPS)).reshape((GROUPS, TARGET_GROUP)).astype(jnp.int32)
    src_doc = jax.vmap(lambda own: jnp.searchsorted(jnp.cumsum(uneven_parts(own, DOCS, SRC_GRP, SRC_GRP // 2, 1)), jnp.arange(SRC_GRP), side="right"))(jax.random.split(keys[4], GROUPS)).reshape((GROUPS, SRC_GRP)).astype(jnp.int32)
    hidden_in = scatter_about(keys[5], (TOKENS, D), 1.0, 6.0, ((0, 64), (1, 8)))
    out_proj = gaussian_with(keys[6], (HD, D), HD ** -0.5, 0.375, ((0, 64), (1, 8)), (0, 1, 64, 4.0))
    norm_gain = jnp.clip(1.0 + 0.18 * jax.random.normal(keys[7], (D,), jnp.float32), 0.1, 1.9)
    router = scatter_about(keys[8], (D, EXPERTS), D ** -0.5, 0.09375, ((0, 8),))
    expert_ids = draw_expert_ids(jax.random.fold_in(keys[13], 71), 0)
    expert_slots = draw_expert_slots(jax.random.fold_in(keys[13], 71), 0)
    w_in = scatter_about(keys[11], (EXPERTS, D, FF), D ** -0.5, 0.09375, ((0, 64), (2, 8)))
    w_out = scatter_about(keys[12], (EXPERTS, FF, D), FF ** -0.5, 0.125, ((0, 64), (1, 8)))
    return {"queries": queries, "src_keys": src_keys, "src_values": src_values, "tgt_doc": tgt_doc, "src_doc": src_doc, "hidden_in": hidden_in, "out_proj": out_proj, "norm_gain": norm_gain, "router": router, "expert_ids": expert_ids, "expert_slots": expert_slots, "w_in": w_in, "w_out": w_out}


def reference(queries, src_keys, src_values, tgt_doc, src_doc, hidden_in, out_proj, norm_gain, router, expert_ids, expert_slots, w_in, w_out):
    groups = tgt_doc.shape[0]
    target_rows = tgt_doc.shape[1]
    source_rows = src_doc.shape[1]
    specialist_room = 2 * target_rows // EXPERTS
    factor = 1.0 / HEAD_DIM ** 0.5
    query_all = queries.reshape(groups, target_rows, HEADS, HEAD_DIM)
    key_all = src_keys.reshape(groups, source_rows, HEADS, HEAD_DIM)
    value_all = src_values.reshape(groups, source_rows, HEADS, HEAD_DIM)
    resid_all = hidden_in.reshape(groups, target_rows, D)
    gain32 = norm_gain.astype(jnp.float32)
    router32 = router.astype(jnp.float32)

    def attend(items):
        query, key, value, target_doc, source_doc, resid, chosen_ids = items
        scores = jnp.einsum('thd,shd->hts', query.astype(jnp.float32), key.astype(jnp.float32)) * factor
        same = target_doc[:, None] == source_doc[None, :]
        scores = jnp.where(same[None], scores, jnp.float32(-1e+30))
        peak = lax.optimization_barrier(jnp.max(scores, axis=2, keepdims=True))
        expo = jnp.exp(scores - peak)
        weights = (expo / lax.optimization_barrier(jnp.sum(expo, axis=2, keepdims=True))).astype(jnp.bfloat16)
        attended = jnp.einsum('hts,shd->thd', weights.astype(jnp.float32), value.astype(jnp.float32))
        attended = attended.astype(jnp.bfloat16).reshape(target_rows, HD)
        mixed = resid.astype(jnp.float32) + jnp.dot(attended, out_proj, preferred_element_type=jnp.float32)
        gated = mixed * gain32
        inverse_rms = lax.rsqrt(lax.optimization_barrier(jnp.sum(mixed * mixed, axis=1)) / D + 1e-06)
        normed = (gated * inverse_rms[:, None]).astype(jnp.bfloat16)
        logits = jnp.dot(gated, router32, precision=lax.Precision.HIGHEST) * inverse_rms[:, None]
        picked = jnp.take_along_axis(logits, chosen_ids[:, None].astype(jnp.int32), axis=1)[:, 0]
        return (mixed, normed, jax.nn.sigmoid(picked))
    mixed_all, normed_all, gate_all = lax.map(attend, (query_all, key_all, value_all, tgt_doc, src_doc, resid_all, expert_ids))
    slot_index = (expert_ids * specialist_room + expert_slots).astype(jnp.int32)
    group_index = jnp.broadcast_to(jnp.arange(groups, dtype=jnp.int32)[:, None], slot_index.shape)
    buffer = jnp.zeros((groups, EXPERTS * specialist_room, D), jnp.bfloat16)
    buffer = buffer.at[group_index, slot_index].set(normed_all)
    buffer = buffer.reshape(groups, EXPERTS, specialist_room, D).transpose(1, 0, 2, 3).reshape(EXPERTS, groups * specialist_room, D)
    block = FF // N_MP

    def expert(items):
        inputs, first, second = items
        pre = jnp.dot(inputs, first, preferred_element_type=jnp.float32)
        hidden = jax.nn.relu(pre).astype(jnp.bfloat16)
        partial_sums = []
        for ordinal_location in range(N_MP):
            part = jnp.dot(hidden[:, ordinal_location * block:(ordinal_location + 1) * block], second[ordinal_location * block:(ordinal_location + 1) * block], preferred_element_type=jnp.float32)
            part = lax.optimization_barrier(part.astype(jnp.bfloat16))
            partial_sums.append(part.astype(jnp.float32))
        return reduce(lambda left, right: left + right, partial_sums).astype(jnp.bfloat16)
    expert_out = lax.map(expert, (buffer, w_in, w_out))
    back = expert_out.reshape(EXPERTS, groups, specialist_room, D).transpose(1, 0, 2, 3).reshape(groups, EXPERTS * specialist_room, D)
    chosen = jax.vmap(lambda rows_b, index_b: jnp.take(rows_b, index_b, axis=0))(back, slot_index)
    result = mixed_all + gate_all[..., None] * chosen.astype(jnp.float32)
    return result.astype(jnp.bfloat16).reshape(groups * target_rows, D)
```

```python
import jax
import jax.numpy as jnp
from jax import lax
from jax.sharding import Mesh, PartitionSpec as P

D = 4096
HEAD_DIM = 64
ROWS = 256
ROOM = 8
EXPERT = ("zl", "y", "c")
MP = ("x", "zh")
BF16 = jnp.bfloat16
F32 = jnp.float32


def exchange(blocks, axes):
    return lax.all_to_all(blocks, axes, split_axis=0, concat_axis=0, tiled=True)


def spread(block, axes, count):
    return exchange(jnp.broadcast_to(block[None], (count,) + block.shape), axes)


def dot32(left, right, dims=(((1,), (0,)), ((), ()))):
    return lax.dot_general(left, right, dims, preferred_element_type=F32)


def body(
    queries,
    src_keys,
    src_values,
    tgt_doc,
    src_doc,
    hidden_in,
    out_proj,
    norm_gain,
    router,
    expert_ids,
    expert_slots,
    w_in,
    w_out,
):
    width = queries.shape[1]
    heads = width // HEAD_DIM
    both = jnp.stack([src_keys.reshape(32, 8, width), src_values.reshape(32, 8, width)])
    both = exchange(both.transpose(2, 0, 1, 3), MP)
    keys = both[:, 0].reshape(ROWS, heads, HEAD_DIM)
    values = both[:, 1].reshape(ROWS, heads, HEAD_DIM)
    first = exchange(w_in[0].reshape(4, 1024, 256), "x")
    second = exchange(w_out[0].reshape(256, 4, 1024).transpose(1, 0, 2), "x")
    proj = spread(out_proj, EXPERT, 64).reshape(2048, 512)

    query_heads = queries.reshape(ROWS, heads, HEAD_DIM)
    scores = jnp.einsum("thd,shd->hts", query_heads, keys, preferred_element_type=F32)
    scores = scores * (1.0 / HEAD_DIM**0.5)
    same = tgt_doc[0][:, None] == src_doc[0][None, :]
    scores = jnp.where(same[None], scores, F32(-1e30))
    peak = jnp.max(scores, axis=2, keepdims=True)
    expo = jnp.exp(scores - peak)
    weights = (expo / jnp.sum(expo, axis=2, keepdims=True)).astype(BF16)
    attended = jnp.einsum("hts,shd->thd", weights, values, preferred_element_type=F32)
    attended = attended.astype(BF16).reshape(ROWS, width)
    attended = spread(attended, MP, 8)
    attended = attended.transpose(1, 0, 2).reshape(ROWS, 8 * width)
    mixed = hidden_in.astype(F32) + dot32(attended, proj)
    gated = mixed * norm_gain

    chosen = expert_ids[0]
    slot = chosen * ROOM + expert_slots[0]
    placing = (lax.broadcasted_iota(jnp.int32, (ROWS, 512), 1) == slot[:, None]).astype(BF16)
    placed = dot32(placing, gated.astype(BF16), (((0,), (0,)), ((), ()))).astype(BF16)
    placed = placed.reshape(1, 64, ROOM, 512)
    received = exchange(
        jnp.broadcast_to(placed, (2, 64, ROOM, 512)).reshape(128, ROOM, 512), ("zh",) + EXPERT
    )
    received = received.reshape(2, 512, 512)

    router32 = router.astype(F32)
    logits = jnp.dot(gated, router32, precision=lax.Precision.HIGHEST)
    column = lax.broadcasted_iota(jnp.int32, (ROWS, 64), 1)
    picked = jnp.sum(jnp.where(column == chosen[:, None], logits, 0.0), axis=1)
    stats = jnp.stack([jnp.sum(mixed * mixed, axis=1), picked])
    stats = jnp.sum(lax.all_gather(stats, MP, axis=0), axis=0)
    inverse_rms = lax.rsqrt(stats[0] / D + 1e-06)
    factor = jax.nn.sigmoid(stats[1] * inverse_rms) * inverse_rms

    first = first.reshape(4, 2, 512, 256)
    pre = jnp.stack(
        [(dot32(received[0], first[i, 0]) + dot32(received[1], first[i, 1])).astype(BF16) for i in range(4)]
    )
    pre = exchange(pre, "x")
    hidden = jax.nn.relu(jnp.sum(pre.astype(F32), axis=0)).astype(BF16)
    hidden = spread(hidden, "x", 4)
    result = sum(dot32(hidden[i], second[i]) for i in range(4)).astype(BF16)
    result = result.reshape(64, ROOM, 2, 512).transpose(2, 0, 1, 3).reshape(128, ROOM, 512)
    returned = exchange(result, ("zh",) + EXPERT).reshape(2, 512, 512)
    rows = dot32(placing, returned[0]) + dot32(placing, returned[1])
    return (mixed + factor[:, None] * rows).astype(BF16)


def solution(mesh):
    fine = Mesh(mesh.devices.reshape(4, 8, 2, 4, 2), EXPERT + MP)
    placed = (
        P(EXPERT, MP),
        P(EXPERT + MP, None),
        P(EXPERT + MP, None),
        P(EXPERT, None),
        P(EXPERT, None),
        P(EXPERT, MP),
        P(EXPERT, MP),
        P(MP),
        P(MP, None),
        P(EXPERT, None),
        P(EXPERT, None),
        P(EXPERT, None, MP),
        P(EXPERT, MP, None),
    )
    return jax.shard_map(
        body, mesh=fine, in_specs=placed, out_specs=P(EXPERT, MP), check_vma=False
    )
```

```python
import jax
import jax.numpy as jnp
from jax import lax
from jax.sharding import Mesh, PartitionSpec as P

D = 4096
HEAD_DIM = 64
ROWS = 256
ROOM = 8
EXPERT = ("zl", "y", "c")
MP = ("x", "zh")
BF16 = jnp.bfloat16
F32 = jnp.float32


def exchange(blocks, axes):
    return lax.all_to_all(blocks, axes, split_axis=0, concat_axis=0, tiled=True)


def spread(block, axes, count):
    return exchange(jnp.broadcast_to(block[None], (count,) + block.shape), axes)


def shift(block, places):
    if places == 0:
        return block
    return lax.ppermute(block, "x", [(i, (i + places) % 4) for i in range(4)])


def dot32(left, right, dims=(((1,), (0,)), ((), ()))):
    return lax.dot_general(left, right, dims, preferred_element_type=F32)


def body(
    queries,
    src_keys,
    src_values,
    tgt_doc,
    src_doc,
    hidden_in,
    out_proj,
    norm_gain,
    router,
    expert_ids,
    expert_slots,
    w_in,
    w_out,
):
    width = queries.shape[1]
    heads = width // HEAD_DIM
    both = jnp.stack([src_keys.reshape(32, 8, width), src_values.reshape(32, 8, width)])
    both = exchange(both.transpose(2, 0, 1, 3), MP)
    keys = both[:, 0].reshape(ROWS, heads, HEAD_DIM)
    values = both[:, 1].reshape(ROWS, heads, HEAD_DIM)
    x = lax.axis_index("x")
    first = [
        shift(lax.dynamic_slice(w_in[0], (1024 * ((x + k) % 4), 0), (1024, 256)), k)
        for k in range(4)
    ]
    half = lax.all_gather(out_proj, "zl", axis=0)
    half = lax.all_gather(half, "y", axis=0)
    other = lax.ppermute(half, "c", [(0, 1), (1, 0)])
    low = lax.axis_index("c") == 0
    proj = jnp.stack([jnp.where(low, half, other), jnp.where(low, other, half)])
    proj = proj.transpose(2, 1, 0, 3, 4).reshape(2048, 512)

    query_heads = queries.reshape(ROWS, heads, HEAD_DIM)
    scores = jnp.einsum("thd,shd->hts", query_heads, keys, preferred_element_type=F32)
    scores = scores * (1.0 / HEAD_DIM**0.5)
    same = tgt_doc[0][:, None] == src_doc[0][None, :]
    scores = jnp.where(same[None], scores, F32(-1e30))
    peak = jnp.max(scores, axis=2, keepdims=True)
    expo = jnp.exp(scores - peak)
    weights = (expo / jnp.sum(expo, axis=2, keepdims=True)).astype(BF16)
    attended = jnp.einsum("hts,shd->thd", weights, values, preferred_element_type=F32)
    attended = attended.astype(BF16).reshape(ROWS, width)
    attended = spread(attended, MP, 8)
    attended = attended.transpose(1, 0, 2).reshape(ROWS, 8 * width)
    mixed = hidden_in.astype(F32) + dot32(attended, proj)
    gated = mixed * norm_gain

    chosen = expert_ids[0]
    slot = chosen * ROOM + expert_slots[0]
    placing = (lax.broadcasted_iota(jnp.int32, (ROWS, 512), 1) == slot[:, None]).astype(BF16)
    placed = dot32(placing, gated.astype(BF16), (((0,), (0,)), ((), ()))).astype(BF16)
    placed = placed.reshape(1, 64, ROOM, 512)
    received = exchange(
        jnp.broadcast_to(placed, (2, 64, ROOM, 512)).reshape(128, ROOM, 512), ("zh",) + EXPERT
    )
    received = received.reshape(2, 512, 512)
    w_out, stat_mixed, placed = lax.optimization_barrier((w_out, mixed, placed))
    second = [
        shift(lax.dynamic_slice(w_out[0], (0, 1024 * ((x + k) % 4)), (256, 1024)), k)
        for k in range(4)
    ]

    router32 = router.astype(F32)
    logits = jnp.dot(stat_mixed * norm_gain, router32, precision=lax.Precision.HIGHEST)
    column = lax.broadcasted_iota(jnp.int32, (ROWS, 64), 1)
    picked = jnp.sum(jnp.where(column == chosen[:, None], logits, 0.0), axis=1)
    stats = jnp.stack([jnp.sum(stat_mixed * stat_mixed, axis=1), picked])
    stats = stats + lax.ppermute(stats, "zh", [(0, 1), (1, 0)])
    stats = stats + lax.ppermute(stats, "x", [(0, 1), (1, 0), (2, 3), (3, 2)])
    stats = stats + lax.ppermute(stats, "x", [(0, 3), (3, 0), (1, 2), (2, 1)])
    inverse_rms = lax.rsqrt(stats[0] / D + 1e-06)
    factor = jax.nn.sigmoid(stats[1] * inverse_rms) * inverse_rms

    pre = [
        (dot32(received[0], first[k][:512]) + dot32(received[1], first[k][512:])).astype(BF16)
        for k in range(4)
    ]
    pre = sum(shift(pre[k], -k).astype(F32) for k in range(4))
    hidden = jax.nn.relu(pre).astype(BF16)
    result = sum(dot32(shift(hidden, k), second[k]) for k in range(4)).astype(BF16)
    result = result.reshape(64, ROOM, 2, 512).transpose(2, 0, 1, 3).reshape(128, ROOM, 512)
    returned = exchange(result, ("zh",) + EXPERT).reshape(2, 512, 512)
    rows = dot32(placing, returned[0]) + dot32(placing, returned[1])
    return (mixed + factor[:, None] * rows).astype(BF16)


def solution(mesh):
    fine = Mesh(mesh.devices.reshape(4, 8, 2, 4, 2), EXPERT + MP)
    placed = (
        P(EXPERT, MP),
        P(EXPERT + MP, None),
        P(EXPERT + MP, None),
        P(EXPERT, None),
        P(EXPERT, None),
        P(EXPERT, MP),
        P(EXPERT, MP),
        P(MP),
        P(MP, None),
        P(EXPERT, None),
        P(EXPERT, None),
        P(EXPERT, None, MP),
        P(EXPERT, MP, None),
    )
    return jax.shard_map(
        body, mesh=fine, in_specs=placed, out_specs=P(EXPERT, MP), check_vma=False
    )
```

```python
import jax
import jax.numpy as jnp
from jax import lax
from jax.experimental import pallas as pl
from jax.experimental.pallas import tpu as pltpu
from jax.sharding import Mesh, PartitionSpec as P

D = 4096
HEAD_DIM = 64
ROWS = 256
ROOM = 8
EXPERT = ("zl", "y", "c")
MP = ("x", "zh")
BF16 = jnp.bfloat16
F32 = jnp.float32


def exchange(blocks, axes):
    return lax.all_to_all(blocks, axes, split_axis=0, concat_axis=0, tiled=True)


def spread(block, axes, count):
    return exchange(jnp.broadcast_to(block[None], (count,) + block.shape), axes)


def shift(block, places):
    if places == 0:
        return block
    return lax.ppermute(block, "x", [(i, (i + places) % 4) for i in range(4)])


def dot32(left, right, dims=(((1,), (0,)), ((), ()))):
    return lax.dot_general(left, right, dims, preferred_element_type=F32)


def pre_kernel(place, rows, own, one, two, three, out):
    for k, weight in enumerate((own, one, two, three)):
        total = dot32(rows[0], weight[:512]) + dot32(rows[1], weight[512:])
        out[(place[0] - k) % 4] = total.astype(BF16)


def hidden_kernel(parts, out):
    total = sum(parts[k].astype(F32) for k in range(4))
    hidden = jnp.maximum(total, 0.0).astype(BF16)
    for k in range(4):
        out[k] = hidden


def result_kernel(place, hidden, own, one, two, three, out):
    blocks = [hidden[(place[0] - k) % 4] for k in range(4)]
    for z in range(2):
        columns = pl.ds(512 * z, 512)
        total = dot32(blocks[0], own[:, columns])
        for k, weight in enumerate((one, two, three)):
            total = total + dot32(blocks[k + 1], weight[:, columns])
        out[z] = total.astype(BF16)


def run(kernel, shape, place, *arrays):
    vmem = pl.BlockSpec(memory_space=pltpu.VMEM)
    smem = pl.BlockSpec(memory_space=pltpu.SMEM)
    flags = [] if place is None else [place]
    return pl.pallas_call(
        kernel,
        out_shape=jax.ShapeDtypeStruct(shape, BF16),
        in_specs=[smem] * len(flags) + [vmem] * len(arrays),
        out_specs=vmem,
        compiler_params=pltpu.CompilerParams(vmem_limit_bytes=16 << 20),
    )(*flags, *arrays)


def body(
    queries,
    src_keys,
    src_values,
    tgt_doc,
    src_doc,
    hidden_in,
    out_proj,
    norm_gain,
    router,
    expert_ids,
    expert_slots,
    w_in,
    w_out,
):
    width = queries.shape[1]
    heads = width // HEAD_DIM
    both = jnp.stack([src_keys.reshape(32, 8, width), src_values.reshape(32, 8, width)])
    both = exchange(both.transpose(2, 0, 1, 3), MP)
    keys = both[:, 0].reshape(ROWS, heads, HEAD_DIM)
    values = both[:, 1].reshape(ROWS, heads, HEAD_DIM)
    x = lax.axis_index("x")
    first = [
        shift(lax.dynamic_slice(w_in[0], (1024 * ((x + k) % 4), 0), (1024, 256)), k)
        for k in range(4)
    ]
    proj = lax.all_gather(out_proj, ("zl", "c"), axis=0, tiled=True)
    proj = lax.all_gather(proj, "y", axis=0)
    proj, first = lax.optimization_barrier((proj, first))
    proj = proj.reshape(8, 4, 64, 512).transpose(1, 0, 2, 3).reshape(2048, 512)

    query_heads = queries.reshape(ROWS, heads, HEAD_DIM)
    scores = jnp.einsum("thd,shd->hts", query_heads, keys, preferred_element_type=F32)
    scores = scores * (1.0 / HEAD_DIM**0.5)
    same = tgt_doc[0][:, None] == src_doc[0][None, :]
    scores = jnp.where(same[None], scores, F32(-1e30))
    peak = jnp.max(scores, axis=2, keepdims=True)
    expo = jnp.exp(scores - peak)
    weights = (expo / jnp.sum(expo, axis=2, keepdims=True)).astype(BF16)
    attended = jnp.einsum("hts,shd->thd", weights, values, preferred_element_type=F32)
    attended = attended.astype(BF16).reshape(ROWS, width)
    attended = spread(attended, MP, 8)
    attended = attended.transpose(1, 0, 2).reshape(ROWS, 8 * width)
    mixed = hidden_in.astype(F32) + dot32(attended, proj)
    gated = mixed * norm_gain

    chosen = expert_ids[0]
    slot = chosen * ROOM + expert_slots[0]
    placing = (lax.broadcasted_iota(jnp.int32, (ROWS, 512), 1) == slot[:, None]).astype(BF16)
    placed = dot32(placing, gated.astype(BF16), (((0,), (0,)), ((), ()))).astype(BF16)
    placed, tied = lax.optimization_barrier((placed, w_out[0]))
    placed = placed.reshape(1, 64, ROOM, 512)
    received = exchange(
        jnp.broadcast_to(placed, (2, 64, ROOM, 512)).reshape(128, ROOM, 512), ("zh",) + EXPERT
    )
    received = received.reshape(2, 512, 512)
    second = [
        shift(lax.dynamic_slice(tied, (0, 1024 * ((x + k) % 4)), (256, 1024)), k)
        for k in range(4)
    ]

    received, second = lax.optimization_barrier((received, second))

    router32 = router.astype(F32)
    logits = jnp.dot(mixed * norm_gain, router32, precision=lax.Precision.HIGHEST)
    column = lax.broadcasted_iota(jnp.int32, (ROWS, 64), 1)
    picked = jnp.sum(jnp.where(column == chosen[:, None], logits, 0.0), axis=1)
    stats = jnp.stack([jnp.sum(mixed * mixed, axis=1), picked])
    stats = stats + lax.ppermute(stats, "zh", [(0, 1), (1, 0)])
    stats = stats + lax.ppermute(stats, "x", [(0, 1), (1, 0), (2, 3), (3, 2)])
    stats = stats + lax.ppermute(stats, "x", [(0, 3), (3, 0), (1, 2), (2, 1)])
    inverse_rms = lax.rsqrt(stats[0] / D + 1e-06)
    factor = jax.nn.sigmoid(stats[1] * inverse_rms) * inverse_rms

    place = x.astype(jnp.int32).reshape(1)
    pre = exchange(run(pre_kernel, (4, 512, 256), place, received, *first), "x")
    hidden = exchange(run(hidden_kernel, (4, 512, 256), None, pre), "x")
    result = run(result_kernel, (2, 512, 512), place, hidden, *second).reshape(128, ROOM, 512)
    returned = exchange(result, ("zh",) + EXPERT).reshape(2, 512, 512)
    rows = dot32(placing, returned[0]) + dot32(placing, returned[1])
    return (mixed + factor[:, None] * rows).astype(BF16)


def solution(mesh):
    fine = Mesh(mesh.devices.reshape(4, 8, 2, 4, 2), EXPERT + MP)
    placed = (
        P(EXPERT, MP),
        P(EXPERT + MP, None),
        P(EXPERT + MP, None),
        P(EXPERT, None),
        P(EXPERT, None),
        P(EXPERT, MP),
        P(EXPERT, MP),
        P(MP),
        P(MP, None),
        P(EXPERT, None),
        P(EXPERT, None),
        P(EXPERT, None, MP),
        P(EXPERT, MP, None),
    )
    return jax.shard_map(
        body, mesh=fine, in_specs=placed, out_specs=P(EXPERT, MP), check_vma=False
    )
```

```python
import jax
import jax.numpy as jnp
from jax import lax
from jax.experimental import pallas as pl
from jax.experimental.pallas import tpu as pltpu
from jax.sharding import Mesh, PartitionSpec as P

D = 4096
HEAD_DIM = 64
ROWS = 256
ROOM = 8
EXPERT = ("zl", "y", "c")
MP = ("x", "zh")
BF16 = jnp.bfloat16
F32 = jnp.float32


def exchange(blocks, axes):
    return lax.all_to_all(blocks, axes, split_axis=0, concat_axis=0, tiled=True)


def spread(block, axes, count):
    return exchange(jnp.broadcast_to(block[None], (count,) + block.shape), axes)


def shift(block, places):
    if places == 0:
        return block
    return lax.ppermute(block, "x", [(i, (i + places) % 4) for i in range(4)])


def dot32(left, right, dims=(((1,), (0,)), ((), ()))):
    return lax.dot_general(left, right, dims, preferred_element_type=F32)


def pre_kernel(place, rows, own, one, two, three, out):
    for k, weight in enumerate((own, one, two, three)):
        total = dot32(rows[0], weight[:512]) + dot32(rows[1], weight[512:])
        out[(place[0] - k) % 4] = total.astype(BF16)


def hidden_kernel(parts, out):
    total = sum(parts[k].astype(F32) for k in range(4))
    hidden = jnp.maximum(total, 0.0).astype(BF16)
    for k in range(4):
        out[k] = hidden


def result_kernel(place, hidden, own, one, two, three, out):
    blocks = [hidden[(place[0] - k) % 4] for k in range(4)]
    for z in range(2):
        columns = pl.ds(512 * z, 512)
        total = dot32(blocks[0], own[:, columns])
        for k, weight in enumerate((one, two, three)):
            total = total + dot32(blocks[k + 1], weight[:, columns])
        out[z] = total.astype(BF16)


def pack_kernel(keys, values, out):
    for k in range(8):
        columns = pl.ds(256 * k, 256)
        out[k, 0] = keys[:, columns]
        out[k, 1] = values[:, columns]


def mix_kernel(attended, proj, hidden_in, gain, slot, mixed, placed, rows):
    for zl in range(4):
        for y in range(8):
            rows[pl.ds(64 * (8 * zl + y), 64)] = proj[y, zl]
    total = hidden_in[...].astype(F32)
    for k in range(8):
        total = total + dot32(attended[k], rows[pl.ds(256 * k, 256)])
    mixed[...] = total
    taken = lax.broadcasted_iota(jnp.int32, (512, ROWS), 0) == slot[...]
    taken = jnp.where(taken, F32(1.0), F32(0.0)).astype(BF16)
    slots = dot32(taken, (total * gain[...]).astype(BF16)).astype(BF16)
    placed[0] = slots
    placed[1] = slots


def run(kernel, shape, place, *arrays):
    vmem = pl.BlockSpec(memory_space=pltpu.VMEM)
    smem = pl.BlockSpec(memory_space=pltpu.SMEM)
    flags = [] if place is None else [place]
    return pl.pallas_call(
        kernel,
        out_shape=jax.ShapeDtypeStruct(shape, BF16),
        in_specs=[smem] * len(flags) + [vmem] * len(arrays),
        out_specs=vmem,
        compiler_params=pltpu.CompilerParams(vmem_limit_bytes=16 << 20),
    )(*flags, *arrays)


def body(
    queries,
    src_keys,
    src_values,
    tgt_doc,
    src_doc,
    hidden_in,
    out_proj,
    norm_gain,
    router,
    expert_ids,
    expert_slots,
    w_in,
    w_out,
):
    width = queries.shape[1]
    heads = width // HEAD_DIM
    both = exchange(run(pack_kernel, (8, 2, 32, width), None, src_keys, src_values), MP)
    keys = both[:, 0].reshape(ROWS, heads, HEAD_DIM)
    values = both[:, 1].reshape(ROWS, heads, HEAD_DIM)
    x = lax.axis_index("x")
    proj = lax.all_gather(out_proj, ("zl", "c"), axis=0, tiled=True)
    proj = lax.all_gather(proj, "y", axis=0)

    query_heads = queries.reshape(ROWS, heads, HEAD_DIM)
    scores = jnp.einsum("thd,shd->hts", query_heads, keys, preferred_element_type=F32)
    scores = scores * (1.0 / HEAD_DIM**0.5)
    same = tgt_doc[0][:, None] == src_doc[0][None, :]
    scores = jnp.where(same[None], scores, F32(-1e30))
    peak = jnp.max(scores, axis=2, keepdims=True)
    expo = jnp.exp(scores - peak)
    weights = (expo / jnp.sum(expo, axis=2, keepdims=True)).astype(BF16)
    attended = jnp.einsum("hts,shd->thd", weights, values, preferred_element_type=F32)
    attended = attended.astype(BF16).reshape(ROWS, width)
    attended = spread(attended, MP, 8)
    chosen = expert_ids[0]
    slot = chosen * ROOM + expert_slots[0]
    placing = (lax.broadcasted_iota(jnp.int32, (ROWS, 512), 1) == slot[:, None]).astype(BF16)
    vmem = pl.BlockSpec(memory_space=pltpu.VMEM)
    mixed, placed = pl.pallas_call(
        mix_kernel,
        out_shape=(
            jax.ShapeDtypeStruct((ROWS, 512), F32),
            jax.ShapeDtypeStruct((2, 512, 512), BF16),
        ),
        in_specs=[vmem] * 5,
        out_specs=(vmem, vmem),
        scratch_shapes=[pltpu.VMEM((2048, 512), BF16)],
        compiler_params=pltpu.CompilerParams(vmem_limit_bytes=24 << 20),
    )(attended, proj.reshape(8, 4, 64, 512), hidden_in, norm_gain.reshape(1, 512), slot.reshape(1, ROWS))
    placed, tied, feeding = lax.optimization_barrier((placed, w_out[0], w_in[0]))
    received = exchange(placed.reshape(128, ROOM, 512), ("zh",) + EXPERT)
    received = received.reshape(2, 512, 512)
    first = [
        shift(lax.dynamic_slice(feeding, (1024 * ((x + k) % 4), 0), (1024, 256)), k)
        for k in range(4)
    ]
    second = [
        shift(lax.dynamic_slice(tied, (0, 1024 * ((x + k) % 4)), (256, 1024)), k)
        for k in range(4)
    ]


    router32 = router.astype(F32)
    logits = jnp.dot(mixed * norm_gain, router32, precision=lax.Precision.HIGHEST)
    column = lax.broadcasted_iota(jnp.int32, (ROWS, 64), 1)
    picked = jnp.sum(jnp.where(column == chosen[:, None], logits, 0.0), axis=1)
    stats = jnp.stack([jnp.sum(mixed * mixed, axis=1), picked])
    stats = stats + lax.ppermute(stats, "zh", [(0, 1), (1, 0)])
    stats = stats + lax.ppermute(stats, "x", [(0, 1), (1, 0), (2, 3), (3, 2)])
    stats = stats + lax.ppermute(stats, "x", [(0, 3), (3, 0), (1, 2), (2, 1)])
    inverse_rms = lax.rsqrt(stats[0] / D + 1e-06)
    factor = jax.nn.sigmoid(stats[1] * inverse_rms) * inverse_rms

    place = x.astype(jnp.int32).reshape(1)
    pre = run(pre_kernel, (4, 512, 256), place, received, *first)
    pre, second[2] = lax.optimization_barrier((pre, second[2]))
    pre = exchange(pre, "x")
    hidden = exchange(run(hidden_kernel, (4, 512, 256), None, pre), "x")
    result = run(result_kernel, (2, 512, 512), place, hidden, *second).reshape(128, ROOM, 512)
    returned = exchange(result, ("zh",) + EXPERT).reshape(2, 512, 512)
    rows = dot32(placing, returned[0]) + dot32(placing, returned[1])
    return (mixed + factor[:, None] * rows).astype(BF16)


def solution(mesh):
    fine = Mesh(mesh.devices.reshape(4, 8, 2, 4, 2), EXPERT + MP)
    placed = (
        P(EXPERT, MP),
        P(EXPERT + MP, None),
        P(EXPERT + MP, None),
        P(EXPERT, None),
        P(EXPERT, None),
        P(EXPERT, MP),
        P(EXPERT, MP),
        P(MP),
        P(MP, None),
        P(EXPERT, None),
        P(EXPERT, None),
        P(EXPERT, None, MP),
        P(EXPERT, MP, None),
    )
    return jax.shard_map(
        body, mesh=fine, in_specs=placed, out_specs=P(EXPERT, MP), check_vma=False
    )
```

```python
import jax
import jax.numpy as jnp
from jax import lax
from jax.experimental import pallas as pl
from jax.experimental.pallas import tpu as pltpu
from jax.sharding import Mesh, PartitionSpec as P

D = 4096
HEAD_DIM = 64
ROWS = 256
ROOM = 8
EXPERT = ("zl", "y", "c")
MP = ("x", "zh")
BF16 = jnp.bfloat16
F32 = jnp.float32


def exchange(blocks, axes):
    return lax.all_to_all(blocks, axes, split_axis=0, concat_axis=0, tiled=True)


def spread(block, axes, count):
    return exchange(jnp.broadcast_to(block[None], (count,) + block.shape), axes)


def shift(block, places):
    if places == 0:
        return block
    return lax.ppermute(block, "x", [(i, (i + places) % 4) for i in range(4)])


def dot32(left, right, dims=(((1,), (0,)), ((), ()))):
    return lax.dot_general(left, right, dims, preferred_element_type=F32)


def fetch(weights, held, done):
    copies = [pltpu.make_async_copy(weights[k], held.at[k], done.at[k]) for k in range(4)]
    for copy in copies:
        copy.start()
    return copies


def pre_kernel(place, rows, own, one, two, three, out, held, done):
    copies = fetch((own, one, two, three), held, done)
    for k in range(4):
        copies[k].wait()
        total = dot32(rows[0], held[k, :512]) + dot32(rows[1], held[k, 512:])
        out[(place[0] - k) % 4] = total.astype(BF16)


def hidden_kernel(parts, out):
    total = sum(parts[k].astype(F32) for k in range(4))
    hidden = jnp.maximum(total, 0.0).astype(BF16)
    for k in range(4):
        out[k] = hidden


def result_kernel(place, hidden, own, one, two, three, out, held, done):
    copies = fetch((own, one, two, three), held, done)
    for copy in copies:
        copy.wait()
    for z in range(2):
        columns = pl.ds(512 * z, 512)
        total = dot32(hidden[place[0]], held[0, :, columns])
        for k in range(1, 4):
            total = total + dot32(hidden[(place[0] - k) % 4], held[k, :, columns])
        out[z] = total.astype(BF16)


def run(kernel, shapes, place, arrays, weights=(), scratch=()):
    vmem = pl.BlockSpec(memory_space=pltpu.VMEM)
    smem = pl.BlockSpec(memory_space=pltpu.SMEM)
    far = pl.BlockSpec(memory_space=pl.ANY)
    flags = [] if place is None else [place]
    scratch = list(scratch)
    if weights:
        scratch = [pltpu.VMEM((4,) + weights[0].shape, BF16), pltpu.SemaphoreType.DMA((4,))]
    return pl.pallas_call(
        kernel,
        out_shape=shapes,
        in_specs=[smem] * len(flags) + [vmem] * len(arrays) + [far] * len(weights),
        out_specs=jax.tree.map(lambda leaf: vmem, shapes),
        scratch_shapes=scratch,
        compiler_params=pltpu.CompilerParams(vmem_limit_bytes=24 << 20),
    )(*flags, *arrays, *weights)


def spot(*dims, dtype=BF16):
    return jax.ShapeDtypeStruct(dims, dtype)


def body(
    queries,
    src_keys,
    src_values,
    tgt_doc,
    src_doc,
    hidden_in,
    out_proj,
    norm_gain,
    router,
    expert_ids,
    expert_slots,
    w_in,
    w_out,
):
    width = queries.shape[1]
    heads = width // HEAD_DIM
    both = jnp.stack([src_keys.reshape(32, 8, width), src_values.reshape(32, 8, width)])
    both = exchange(both.transpose(2, 0, 1, 3), MP)
    keys = both[:, 0].reshape(ROWS, heads, HEAD_DIM)
    values = both[:, 1].reshape(ROWS, heads, HEAD_DIM)
    x = lax.axis_index("x")
    first = [
        shift(lax.dynamic_slice(w_in[0], (1024 * ((x + k) % 4), 0), (1024, 256)), k)
        for k in range(4)
    ]
    half = lax.all_gather(out_proj, "zl", axis=0)
    half = lax.all_gather(half, "y", axis=0)
    half, first = lax.optimization_barrier((half, first))
    other = lax.ppermute(half, "c", [(0, 1), (1, 0)])
    low = lax.axis_index("c") == 0
    proj = jnp.stack([jnp.where(low, half, other), jnp.where(low, other, half)])
    proj = proj.transpose(2, 1, 0, 3, 4).reshape(2048, 512)

    query_heads = queries.reshape(ROWS, heads, HEAD_DIM)
    scores = jnp.einsum("thd,shd->hts", query_heads, keys, preferred_element_type=F32)
    scores = scores * (1.0 / HEAD_DIM**0.5)
    same = tgt_doc[0][:, None] == src_doc[0][None, :]
    scores = jnp.where(same[None], scores, F32(-1e30))
    peak = jnp.max(scores, axis=2, keepdims=True)
    expo = jnp.exp(scores - peak)
    weights = (expo / jnp.sum(expo, axis=2, keepdims=True)).astype(BF16)
    attended = jnp.einsum("hts,shd->thd", weights, values, preferred_element_type=F32)
    attended = attended.astype(BF16).reshape(ROWS, width)
    attended = spread(attended, MP, 8)
    attended = attended.transpose(1, 0, 2).reshape(ROWS, 8 * width)
    mixed = hidden_in.astype(F32) + dot32(attended, proj)
    gated = mixed * norm_gain

    chosen = expert_ids[0]
    slot = chosen * ROOM + expert_slots[0]
    placing = (lax.broadcasted_iota(jnp.int32, (ROWS, 512), 1) == slot[:, None]).astype(BF16)
    placed = dot32(placing, gated.astype(BF16), (((0,), (0,)), ((), ()))).astype(BF16)
    placed, tied = lax.optimization_barrier((placed, w_out[0]))
    placed = placed.reshape(1, 64, ROOM, 512)
    received = exchange(
        jnp.broadcast_to(placed, (2, 64, ROOM, 512)).reshape(128, ROOM, 512), ("zh",) + EXPERT
    )
    received = received.reshape(2, 512, 512)
    second = [
        shift(lax.dynamic_slice(tied, (0, 1024 * ((x + k) % 4)), (256, 1024)), k)
        for k in range(4)
    ]

    router32 = router.astype(F32)
    logits = jnp.dot(mixed * norm_gain, router32, precision=lax.Precision.HIGHEST)
    column = lax.broadcasted_iota(jnp.int32, (ROWS, 64), 1)
    picked = jnp.sum(jnp.where(column == chosen[:, None], logits, 0.0), axis=1)
    stats = jnp.stack([jnp.sum(mixed * mixed, axis=1), picked])
    stats = stats + lax.ppermute(stats, "zh", [(0, 1), (1, 0)])
    stats = stats + lax.ppermute(stats, "x", [(0, 1), (1, 0), (2, 3), (3, 2)])
    stats = stats + lax.ppermute(stats, "x", [(0, 3), (3, 0), (1, 2), (2, 1)])
    inverse_rms = lax.rsqrt(stats[0] / D + 1e-06)
    factor = jax.nn.sigmoid(stats[1] * inverse_rms) * inverse_rms

    place = x.astype(jnp.int32).reshape(1)
    pre = run(pre_kernel, spot(4, 512, 256), place, [received], first)
    pre, second = lax.optimization_barrier((pre, second))
    hidden = exchange(run(hidden_kernel, spot(4, 512, 256), None, [exchange(pre, "x")]), "x")
    result = run(result_kernel, spot(2, 512, 512), place, [hidden], second)
    result = result.reshape(128, ROOM, 512)
    returned = exchange(result, ("zh",) + EXPERT).reshape(2, 512, 512)
    rows = dot32(placing, returned[0]) + dot32(placing, returned[1])
    return (mixed + factor[:, None] * rows).astype(BF16)


def solution(mesh):
    fine = Mesh(mesh.devices.reshape(4, 8, 2, 4, 2), EXPERT + MP)
    placed = (
        P(EXPERT, MP),
        P(EXPERT + MP, None),
        P(EXPERT + MP, None),
        P(EXPERT, None),
        P(EXPERT, None),
        P(EXPERT, MP),
        P(EXPERT, MP),
        P(MP),
        P(MP, None),
        P(EXPERT, None),
        P(EXPERT, None),
        P(EXPERT, None, MP),
        P(EXPERT, MP, None),
    )
    return jax.shard_map(
        body, mesh=fine, in_specs=placed, out_specs=P(EXPERT, MP), check_vma=False
    )
```

```python
import jax
import jax.numpy as jnp
from jax import lax
from jax.experimental import pallas as pl
from jax.experimental.pallas import tpu as pltpu
from jax.sharding import Mesh, PartitionSpec as P

D = 4096
HEAD_DIM = 64
ROWS = 256
ROOM = 8
EXPERT = ("zl", "y", "c")
MP = ("x", "zh")
BF16 = jnp.bfloat16
F32 = jnp.float32


def exchange(blocks, axes):
    return lax.all_to_all(blocks, axes, split_axis=0, concat_axis=0, tiled=True)


def spread(block, axes, count):
    return exchange(jnp.broadcast_to(block[None], (count,) + block.shape), axes)


def shift(block, places):
    if places == 0:
        return block
    return lax.ppermute(block, "x", [(i, (i + places) % 4) for i in range(4)])


def dot32(left, right, dims=(((1,), (0,)), ((), ()))):
    return lax.dot_general(left, right, dims, preferred_element_type=F32)


def fetch(weights, held, done):
    copies = [pltpu.make_async_copy(weights[k], held.at[k], done.at[k]) for k in range(4)]
    for copy in copies:
        copy.start()
    return copies


def pre_kernel(place, rows, own, one, two, three, out):
    for k, weight in enumerate((own, one, two, three)):
        total = dot32(rows[0], weight[:512]) + dot32(rows[1], weight[512:])
        out[(place[0] - k) % 4] = total.astype(BF16)


def hidden_kernel(parts, out):
    total = sum(parts[k].astype(F32) for k in range(4))
    hidden = jnp.maximum(total, 0.0).astype(BF16)
    for k in range(4):
        out[k] = hidden


def result_kernel(place, hidden, own, one, two, three, out, held, done):
    copies = fetch((own, one, two, three), held, done)
    for copy in copies:
        copy.wait()
    for z in range(2):
        columns = pl.ds(512 * z, 512)
        total = dot32(hidden[place[0]], held[0, :, columns])
        for k in range(1, 4):
            total = total + dot32(hidden[(place[0] - k) % 4], held[k, :, columns])
        out[z] = total.astype(BF16)


def run(kernel, shapes, place, arrays, weights=(), scratch=()):
    vmem = pl.BlockSpec(memory_space=pltpu.VMEM)
    smem = pl.BlockSpec(memory_space=pltpu.SMEM)
    far = pl.BlockSpec(memory_space=pl.ANY)
    flags = [] if place is None else [place]
    scratch = list(scratch)
    if weights:
        scratch = [pltpu.VMEM((4,) + weights[0].shape, BF16), pltpu.SemaphoreType.DMA((4,))]
    return pl.pallas_call(
        kernel,
        out_shape=shapes,
        in_specs=[smem] * len(flags) + [vmem] * len(arrays) + [far] * len(weights),
        out_specs=jax.tree.map(lambda leaf: vmem, shapes),
        scratch_shapes=scratch,
        compiler_params=pltpu.CompilerParams(vmem_limit_bytes=24 << 20),
    )(*flags, *arrays, *weights)


def spot(*dims, dtype=BF16):
    return jax.ShapeDtypeStruct(dims, dtype)


def body(
    queries,
    src_keys,
    src_values,
    tgt_doc,
    src_doc,
    hidden_in,
    out_proj,
    norm_gain,
    router,
    expert_ids,
    expert_slots,
    w_in,
    w_out,
):
    width = queries.shape[1]
    heads = width // HEAD_DIM
    both = jnp.stack([src_keys.reshape(32, 8, width), src_values.reshape(32, 8, width)])
    both = exchange(both.transpose(2, 0, 1, 3), MP)
    keys = both[:, 0].reshape(ROWS, heads, HEAD_DIM)
    values = both[:, 1].reshape(ROWS, heads, HEAD_DIM)
    x = lax.axis_index("x")
    first = [
        shift(lax.dynamic_slice(w_in[0], (1024 * ((x + k) % 4), 0), (1024, 256)), k)
        for k in range(4)
    ]
    half = lax.all_gather(out_proj, "zl", axis=0)
    half = lax.all_gather(half, "y", axis=0)
    half, first = lax.optimization_barrier((half, first))
    other = lax.ppermute(half, "c", [(0, 1), (1, 0)])
    low = lax.axis_index("c") == 0
    proj = jnp.stack([jnp.where(low, half, other), jnp.where(low, other, half)])
    proj = proj.transpose(2, 1, 0, 3, 4).reshape(2048, 512)

    query_heads = queries.reshape(ROWS, heads, HEAD_DIM)
    scores = jnp.einsum("thd,shd->hts", query_heads, keys, preferred_element_type=F32)
    scores = scores * (1.0 / HEAD_DIM**0.5)
    same = tgt_doc[0][:, None] == src_doc[0][None, :]
    scores = jnp.where(same[None], scores, F32(-1e30))
    peak = jnp.max(scores, axis=2, keepdims=True)
    expo = jnp.exp(scores - peak)
    weights = (expo / jnp.sum(expo, axis=2, keepdims=True)).astype(BF16)
    attended = jnp.einsum("hts,shd->thd", weights, values, preferred_element_type=F32)
    attended = attended.astype(BF16).reshape(ROWS, width)
    attended = spread(attended, MP, 8)
    attended = attended.transpose(1, 0, 2).reshape(ROWS, 8 * width)
    mixed = hidden_in.astype(F32) + dot32(attended, proj)
    gated = mixed * norm_gain

    chosen = expert_ids[0]
    slot = chosen * ROOM + expert_slots[0]
    placing = (lax.broadcasted_iota(jnp.int32, (ROWS, 512), 1) == slot[:, None]).astype(BF16)
    placed = dot32(placing, gated.astype(BF16), (((0,), (0,)), ((), ()))).astype(BF16)
    placed, tied = lax.optimization_barrier((placed, w_out[0]))
    placed = placed.reshape(1, 64, ROOM, 512)
    received = exchange(
        jnp.broadcast_to(placed, (2, 64, ROOM, 512)).reshape(128, ROOM, 512), ("zh",) + EXPERT
    )
    received = received.reshape(2, 512, 512)
    second = [
        shift(lax.dynamic_slice(tied, (0, 1024 * ((x + k) % 4)), (256, 1024)), k)
        for k in range(4)
    ]

    router32 = router.astype(F32)
    logits = jnp.dot(mixed * norm_gain, router32, precision=lax.Precision.HIGHEST)
    column = lax.broadcasted_iota(jnp.int32, (ROWS, 64), 1)
    picked = jnp.sum(jnp.where(column == chosen[:, None], logits, 0.0), axis=1)
    stats = jnp.stack([jnp.sum(mixed * mixed, axis=1), picked])
    stats = stats + lax.ppermute(stats, "zh", [(0, 1), (1, 0)])
    stats = stats + lax.ppermute(stats, "x", [(0, 1), (1, 0), (2, 3), (3, 2)])
    stats = stats + lax.ppermute(stats, "x", [(0, 3), (3, 0), (1, 2), (2, 1)])
    inverse_rms = lax.rsqrt(stats[0] / D + 1e-06)
    factor = jax.nn.sigmoid(stats[1] * inverse_rms) * inverse_rms

    place = x.astype(jnp.int32).reshape(1)
    pre = run(pre_kernel, spot(4, 512, 256), place, [received, *first])
    pre, second = lax.optimization_barrier((pre, second))
    hidden = exchange(run(hidden_kernel, spot(4, 512, 256), None, [exchange(pre, "x")]), "x")
    result = run(result_kernel, spot(2, 512, 512), place, [hidden], second)
    result = result.reshape(128, ROOM, 512)
    returned = exchange(result, ("zh",) + EXPERT).reshape(2, 512, 512)
    rows = dot32(placing, returned[0]) + dot32(placing, returned[1])
    return (mixed + factor[:, None] * rows).astype(BF16)


def solution(mesh):
    fine = Mesh(mesh.devices.reshape(4, 8, 2, 4, 2), EXPERT + MP)
    placed = (
        P(EXPERT, MP),
        P(EXPERT + MP, None),
        P(EXPERT + MP, None),
        P(EXPERT, None),
        P(EXPERT, None),
        P(EXPERT, MP),
        P(EXPERT, MP),
        P(MP),
        P(MP, None),
        P(EXPERT, None),
        P(EXPERT, None),
        P(EXPERT, None, MP),
        P(EXPERT, MP, None),
    )
    return jax.shard_map(
        body, mesh=fine, in_specs=placed, out_specs=P(EXPERT, MP), check_vma=False
    )
```
